32 devices in a mesh: group: 4 (over x, core), head: 8 (over z, y).
Axes of the slice: x: 2, y: 2, z: 4, core: 2. Of those that a mesh axis runs over, the one named last changes fastest.
Arguments:
- queries: bfloat16 [4, 1024, 4096], P('group', 'head')
- keys: bfloat16 [4, 1024, 4096], P('group', 'head')
- values: bfloat16 [4, 1024, 4096], P('group', 'head'), may hold values from -6 to 6
- group_mask: int32 [4, 4, 32], replicated, may hold values from 0 to 1, as said below
- noise_level: int32 [4], replicated, may hold values from 0 to 7
- token_count: int32 [4], replicated, may hold values from 512 to 1024, as said below
- level_gate: float32 [8, 4096], replicated, may hold values from 0.5 to 2
Outputs:
- gated: bfloat16 [4, 1024, 4096], P('group', 'head')
The draws below stay inside these ranges and needn't reach their ends.
Inputs may be any that keep to these rules, and one draw needn't show every extreme that they name: group_mask[c, c, h] = 1; group_mask[c, e, h] = 0 where e > c or c - e >= 3; the last group attends in every head to all 3 groups it may. `token_count`: some group has all 1024 tokens live.
All inputs are finite; a program needn't handle non-finite values.
Results may differ from the reference program's by a relative error of at most 0.0048.
Values may be sent and summed in bfloat16 or wider, within the bound.
A program may use at most 128 MiB of HBM per device.

```python
import jax
import jax.numpy as jnp
from jax import lax

HEADS = 32
HD = 128
HH = 4096
GROUPS = 4
SEQ = 1024
WIN = 3
LEVELS = 8


def draw_queries(key, part):
    key = jax.random.fold_in(key, 11)
    drawn = jax.random.normal(key, (GROUPS, SEQ, HEADS * HD), jnp.float32)
    return drawn.astype(jnp.bfloat16)


def draw_keys(key, part):
    key = jax.random.fold_in(key, 12)
    drawn = jax.random.normal(key, (GROUPS, SEQ, HEADS * HD), jnp.float32)
    return drawn.astype(jnp.bfloat16)


def draw_group_mask(key, part):
    key = jax.random.fold_in(key, 21)
    random_bits = jax.random.randint(key, (GROUPS, GROUPS, HEADS), 0, 2)
    rows = jnp.arange(GROUPS)[:, None, None]
    columns = jnp.arange(GROUPS)[None, :, None]
    lagged = rows - columns
    inside = (lagged >= 1) & (lagged < WIN)
    result = jnp.where(lagged == 0, 1, jnp.where(inside, random_bits, 0))
    result = jnp.where((rows == GROUPS - 1) & inside, 1, result)
    return result.astype(jnp.int32)


def draw_token_count(key, part):
    key = jax.random.fold_in(key, 31)
    counted = jax.random.randint(key, (GROUPS,), SEQ // 2, SEQ + 1)
    filled = jax.random.randint(jax.random.fold_in(key, 1), (), 0, GROUPS)
    return jnp.where(jnp.arange(GROUPS) == filled, SEQ, counted).astype(jnp.int32)


def place_ends(values, key, smallest, top_value):
    shape = values.shape
    spot = [jax.random.randint(jax.random.fold_in(key, axis), (), 0, shape[axis]) for axis in range(len(shape))]
    values = values.at[tuple(spot)].set(smallest)
    longest = shape.index(max(shape))
    spot[longest] = (spot[longest] + 1) % shape[longest]
    return values.at[tuple(spot)].set(top_value)


def block_levels(rng, dims, pieces, least, high):
    loudness = 1.0
    for dim, blocks in pieces:
        draws = jax.random.uniform(jax.random.fold_in(jax.random.fold_in(rng, 6), dim), (blocks,), jnp.float32, least / len(pieces), high / len(pieces))
        loudness = loudness * jnp.repeat(jnp.exp(draws), dims[dim] // blocks).reshape((-1,) + (1,) * (len(dims) - 1 - dim))
    return loudness


def centred(rng, extent, spread, most, cuts=(), held_as=jnp.bfloat16):
    values = spread * jax.random.normal(rng, extent, jnp.float32)
    if cuts:
        values = values * block_levels(rng, extent, cuts, -0.22, 0.18)
    return jnp.clip(values, -most, most).astype(held_as)


def setup_inputs(seed: int = 0) -> dict:
    splits = jax.random.split(jax.random.key(seed), 8)
    return {
        "queries": draw_queries(jax.random.fold_in(splits[7], 71), 0),
        "keys": draw_keys(jax.random.fold_in(splits[7], 71), 0),
        "values": centred(splits[2], (GROUPS, SEQ, HH), 1.0, 6.0, ((0, 4), (1, 8))),
        "group_mask": draw_group_mask(jax.random.fold_in(splits[7], 71), 0),
        "noise_level": place_ends(jax.random.randint(splits[4], (GROUPS,), 0, LEVELS), jax.random.fold_in(splits[4], 1), 0, LEVELS - 1).astype(jnp.int32),
        "token_count": draw_token_count(jax.random.fold_in(splits[7], 71), 0),
        "level_gate": jnp.clip(jax.random.uniform(splits[6], (LEVELS, HH), jnp.float32, 0.5, 2.0), 0.5, 2.0),
    }


NEG = -1e30


def block_stats(query_rows, key_rows, value_rows, valid_keys, active):
    scores = jnp.dot(query_rows, key_rows.T, preferred_element_type=jnp.float32) * (HD ** -0.5)
    scores = jnp.where(valid_keys[None, :], scores, NEG)
    block_max = jnp.max(scores, axis=1)
    weights = jnp.where(valid_keys[None, :], jnp.exp(scores - block_max[:, None]), 0.0)
    totals = jnp.sum(weights, axis=1)
    partial_out = jnp.dot(weights.astype(jnp.bfloat16), value_rows, preferred_element_type=jnp.float32)
    block_max = jnp.where(active, block_max, NEG)
    totals = jnp.where(active, totals, 0.0)
    partial_out = jnp.where(active, partial_out, 0.0)
    return block_max, totals, partial_out


def combine(first_stats, second_stats):
    max_one, total_one, out_one = first_stats
    max_two, total_two, out_two = second_stats
    joint = jnp.maximum(max_one, max_two)
    scale_one = jnp.exp(max_one - joint)
    scale_two = jnp.exp(max_two - joint)
    return (joint, scale_one * total_one + scale_two * total_two,
            scale_one[..., None] * out_one + scale_two[..., None] * out_two)


def reference(queries, keys, values, group_mask, noise_level, token_count, level_gate):
    positions = jnp.arange(SEQ)
    head_numbers = jnp.arange(HEADS).astype(jnp.int32)
    results = []
    for target in range(GROUPS):
        earliest = max(0, target - WIN + 1)
        blocks = target + 1 - earliest
        query_heads = queries[target].reshape(SEQ, HEADS, HD).transpose(1, 0, 2)
        key_heads = keys[earliest:target + 1].reshape(blocks, SEQ, HEADS, HD).transpose(2, 0, 1, 3)
        value_heads = values[earliest:target + 1].reshape(blocks, SEQ, HEADS, HD).transpose(2, 0, 1, 3)

        def per_head(operands, target=target, earliest=earliest, blocks=blocks):
            head_number, query_rows, key_stack, value_stack = operands
            carried = (jnp.full((SEQ,), NEG, jnp.float32), jnp.zeros((SEQ,), jnp.float32),
                       jnp.zeros((SEQ, HD), jnp.float32))
            for offset in range(blocks):
                source = earliest + offset
                valid_keys = positions < token_count[source]
                active = group_mask[target, source, head_number] == 1
                carried = combine(carried, block_stats(query_rows, key_stack[offset], value_stack[offset], valid_keys, active))
            return carried[2] / carried[1][:, None]

        attended = lax.map(per_head, (head_numbers, query_heads, key_heads, value_heads))
        attended = attended.transpose(1, 0, 2).reshape(SEQ, HEADS * HD)
        results.append((attended * level_gate[noise_level[target]]).astype(jnp.bfloat16))
    return jnp.stack(results)
```

```python
import functools
import math

import jax
import jax.numpy as jnp
from jax import lax
from jax.experimental import pallas as pl
from jax.experimental.pallas import tpu as pltpu
from jax.sharding import PartitionSpec as P

HD = 128
WIN = 3
AHEAD = 2
MESH = pl.DeviceIdType.MESH


def kernel(
    n, groups, tile,
    q_ref, k_ref, v_ref, mask_ref, level_ref, count_ref, gate_ref, out_ref,
    qbuf, kvbuf, slots, kall, vall, obuf,
    kv_send, kv_recv, q_send, q_recv, slot_send, slot_recv, out_send, out_recv,
):
    group = lax.axis_index("group")
    me = lax.axis_index("head")
    heads, seq, _ = qbuf.shape
    tokens = seq // n
    half = n // 2
    has_next = group < groups - 1
    per = tile // tokens
    n_tiles = seq // tile
    scale = HD ** -0.5 * math.log2(math.e)
    mine = pl.ds(pl.multiple_of(me * tokens, tokens), tokens)

    def columns(place, head):
        return pl.ds(pl.multiple_of((place * heads + head) * HD, HD), HD)

    barrier = pltpu.get_barrier_semaphore()

    def greet(step, carry):
        pl.semaphore_signal(
            barrier, inc=1, device_id={"head": lax.rem(me + step, n)}, device_id_type=MESH
        )
        return carry

    lax.fori_loop(1, n, greet, 0)

    @pl.when(has_next)
    def _():
        pl.semaphore_signal(barrier, inc=1, device_id={"group": group + 1}, device_id_type=MESH)

    @pl.when(group >= 1)
    def _():
        pl.semaphore_signal(barrier, inc=1, device_id={"group": group - 1}, device_id_type=MESH)

    beside = jnp.minimum(group, 1) + jnp.minimum(groups - 1 - group, 1)
    pl.semaphore_wait(barrier, n - 1 + beside)

    def scatter(head, pairs, send_sem, recv_sem):
        for source, target in pairs:
            pltpu.make_async_copy(
                source.at[0, :, columns(me, head)], target.at[mine, :], recv_sem
            ).start()

        def body(step, carry):
            odd = step % 2
            shift = odd * ((step + 1) // 2) + (1 - odd) * (half + step // 2)
            place = lax.rem(me + shift, n)
            for source, target in pairs:
                pltpu.make_async_remote_copy(
                    src_ref=source.at[0, :, columns(place, head)],
                    dst_ref=target.at[mine, :],
                    send_sem=send_sem,
                    recv_sem=recv_sem,
                    device_id={"head": place},
                    device_id_type=MESH,
                ).start()
            return carry

        lax.fori_loop(0, n - 1, body, 0)

    def send_head(head):
        scatter(
            head,
            ((k_ref, kvbuf.at[head, 0]), (v_ref, kvbuf.at[head, 1])),
            kv_send.at[head],
            kv_recv.at[head],
        )
        scatter(head, ((q_ref, qbuf.at[head]),), q_send.at[head], q_recv.at[head])

    def wait_sent(head):
        sent = pl.ds(0, (n - 1) * tokens)
        kv = kvbuf.at[head, :, sent, :]
        pltpu.make_async_copy(kv, kv, kv_send.at[head]).wait()
        q = qbuf.at[head, sent, :]
        pltpu.make_async_copy(q, q, q_send.at[head]).wait()

    def hand_on(head, slot):
        return pltpu.make_async_remote_copy(
            src_ref=kvbuf.at[head] if slot == 0 else slots.at[slot - 1, head],
            dst_ref=slots.at[slot, head],
            send_sem=slot_send.at[slot, head],
            recv_sem=slot_recv.at[slot, head],
            device_id={"group": group + 1},
            device_id_type=MESH,
        )

    def compute(head):
        head_number = me * heads + head
        first_key = kvbuf[head, 0, 0:16, :].astype(jnp.float32)[0:1, :]
        positions = lax.broadcasted_iota(jnp.int32, (seq, HD), 0)
        for offset in range(WIN):
            source = jnp.maximum(group - offset, 0)
            live = jnp.where(
                group >= offset, count_ref[source] * mask_ref[group, source, head_number], 0
            )
            valid = positions < live
            block = kvbuf.at[head] if offset == 0 else slots.at[offset - 1, head]
            rows = pl.ds(offset * seq, seq)
            kall[rows, :] = jnp.where(
                valid, block[0].astype(jnp.float32), first_key
            ).astype(jnp.bfloat16)
            vall[rows, 0:HD] = jnp.where(valid, block[1].astype(jnp.float32), 0.0).astype(
                jnp.bfloat16
            )
            vall[rows, HD : 2 * HD] = jnp.where(valid, 1.0, 0.0).astype(jnp.bfloat16)
        gates = gate_ref[:, columns(me, head)]
        levels = lax.broadcasted_iota(jnp.int32, gates.shape, 0)
        gate = jnp.sum(
            jnp.where(levels == level_ref[group], gates, 0.0), axis=0, keepdims=True
        )

        def body(step, carry):
            index = lax.rem(step + me // per + n_tiles // 2, n_tiles)
            start = pl.multiple_of(index * tile, tile)
            scores = lax.dot_general(
                qbuf[head, pl.ds(start, tile), :],
                kall[...],
                (((1,), (1,)), ((), ())),
                preferred_element_type=jnp.float32,
            )
            top = jnp.max(scores, axis=1, keepdims=True)
            weights = jnp.exp2((scores - top) * scale).astype(jnp.bfloat16)
            summed = jnp.dot(weights, vall[...], preferred_element_type=jnp.float32)
            gated = summed[:, 0:HD] / summed[:, HD : 2 * HD] * gate
            obuf[head, pl.ds(start, tile), :] = gated.astype(jnp.bfloat16)
            for piece in range(per):
                place = index * per + piece
                piece_rows = pl.ds(pl.multiple_of(place * tokens, tokens), tokens)
                finished = obuf.at[head, piece_rows, :]
                landing = out_ref.at[0, :, columns(me, head)]

                @pl.when(place == me)
                def _():
                    pltpu.make_async_copy(finished, landing, out_recv).start()

                @pl.when(place != me)
                def _():
                    pltpu.make_async_remote_copy(
                        src_ref=finished,
                        dst_ref=landing,
                        send_sem=out_send,
                        recv_sem=out_recv,
                        device_id={"head": place},
                        device_id_type=MESH,
                    ).start()

            return carry

        lax.fori_loop(0, n_tiles, body, 0)

    for head in range(min(AHEAD, heads)):
        send_head(head)
    for stage in range(heads + 1):
        if stage < heads:
            pltpu.make_async_copy(kvbuf.at[stage], kvbuf.at[stage], kv_recv.at[stage]).wait()

            @pl.when(has_next)
            def _():
                hand_on(stage, 0).start()

            if stage + AHEAD < heads:
                wait_sent(stage)
                send_head(stage + AHEAD)

            @pl.when(group >= 1)
            def _():
                hand_on(stage, 0).wait_recv()

                @pl.when(has_next)
                def _():
                    hand_on(stage, 1).start()

        if stage >= 1:
            head = stage - 1
            pltpu.make_async_copy(qbuf.at[head], qbuf.at[head], q_recv.at[head]).wait()

            @pl.when(group >= 2)
            def _():
                hand_on(head, 1).wait_recv()

            compute(head)

    for head in range(heads):
        if head + AHEAD >= heads:
            wait_sent(head)

        @pl.when(has_next)
        def _():
            hand_on(head, 0).wait_send()

            @pl.when(group >= 1)
            def _():
                hand_on(head, 1).wait_send()

    sent = obuf.at[:, pl.ds(0, (n - 1) * tokens), :]
    pltpu.make_async_copy(sent, sent, out_send).wait()
    pltpu.make_async_copy(out_ref, out_ref, out_recv).wait()


def solution(mesh):
    n = mesh.shape["head"]
    groups = mesh.shape["group"]

    def shards(queries, keys, values, group_mask, noise_level, token_count, level_gate):
        _, tokens, features = queries.shape
        heads = features // HD // n
        seq = tokens * n
        tile = max(tokens, 256 if seq <= 1024 else 128)
        any_space = pl.BlockSpec(memory_space=pl.ANY)
        smem = pl.BlockSpec(memory_space=pltpu.SMEM)
        dma = pltpu.SemaphoreType.DMA
        scores = heads * seq * seq * WIN
        return pl.pallas_call(
            functools.partial(kernel, n, groups, tile),
            out_shape=jax.ShapeDtypeStruct(queries.shape, jnp.bfloat16),
            in_specs=[any_space] * 3 + [smem] * 3 + [pl.BlockSpec(memory_space=pltpu.VMEM)],
            out_specs=any_space,
            scratch_shapes=[
                pltpu.VMEM((heads, seq, HD), jnp.bfloat16),
                pltpu.VMEM((heads, 2, seq, HD), jnp.bfloat16),
                pltpu.VMEM((WIN - 1, heads, 2, seq, HD), jnp.bfloat16),
                pltpu.VMEM((WIN * seq, HD), jnp.bfloat16),
                pltpu.VMEM((WIN * seq, 2 * HD), jnp.bfloat16),
                pltpu.VMEM((heads, seq, HD), jnp.bfloat16),
                dma((heads,)),
                dma((heads,)),
                dma((heads,)),
                dma((heads,)),
                dma((WIN - 1, heads)),
                dma((WIN - 1, heads)),
                dma,
                dma,
            ],
            compiler_params=pltpu.CompilerParams(
                collective_id=0, has_side_effects=True, vmem_limit_bytes=56 * 1024 * 1024
            ),
            cost_estimate=pl.CostEstimate(
                flops=scores * HD * 4, bytes_accessed=queries.size * 8, transcendentals=scores
            ),
        )(queries, keys, values, group_mask, noise_level, token_count, level_gate)

    return jax.shard_map(
        shards,
        mesh=mesh,
        in_specs=(P("group", "head", None),) * 3 + (P(),) * 4,
        out_specs=P("group", "head", None),
        check_vma=False,
    )
```

```python
import functools
import math

import jax
import jax.numpy as jnp
from jax import lax
from jax.experimental import pallas as pl
from jax.experimental.pallas import tpu as pltpu
from jax.sharding import PartitionSpec as P

HD = 128
WIN = 3
AHEAD = 4
MESH = pl.DeviceIdType.MESH


def kernel(
    n, groups, tile,
    q_ref, k_ref, v_ref, mask_ref, level_ref, count_ref, gate_ref, out_ref,
    qbuf, kvbuf, slots, kall, vall, obuf,
    kv_send, kv_recv, q_send, q_recv, slot_send, slot_recv, out_send, out_recv,
):
    group = lax.axis_index("group")
    me = lax.axis_index("head")
    heads, seq, _ = qbuf.shape
    tokens = seq // n
    half = n // 2
    has_next = group < groups - 1
    per = tile // tokens
    n_tiles = seq // tile
    scale = HD ** -0.5 * math.log2(math.e)
    mine = pl.ds(pl.multiple_of(me * tokens, tokens), tokens)

    def columns(place, head):
        return pl.ds(pl.multiple_of((place * heads + head) * HD, HD), HD)

    barrier = pltpu.get_barrier_semaphore()

    def greet(step, carry):
        pl.semaphore_signal(
            barrier, inc=1, device_id={"head": lax.rem(me + step, n)}, device_id_type=MESH
        )
        return carry

    lax.fori_loop(1, n, greet, 0)

    @pl.when(has_next)
    def _():
        pl.semaphore_signal(barrier, inc=1, device_id={"group": group + 1}, device_id_type=MESH)

    @pl.when(group >= 1)
    def _():
        pl.semaphore_signal(barrier, inc=1, device_id={"group": group - 1}, device_id_type=MESH)

    beside = jnp.minimum(group, 1) + jnp.minimum(groups - 1 - group, 1)
    pl.semaphore_wait(barrier, n - 1 + beside)

    def scatter(head, pairs, send_sem, recv_sem):
        for source, target in pairs:
            pltpu.make_async_copy(
                source.at[0, :, columns(me, head)], target.at[mine, :], recv_sem
            ).start()

        def body(step, carry):
            odd = step % 2
            shift = odd * ((step + 1) // 2) + (1 - odd) * (half + step // 2)
            place = lax.rem(me + shift, n)
            for source, target in pairs:
                pltpu.make_async_remote_copy(
                    src_ref=source.at[0, :, columns(place, head)],
                    dst_ref=target.at[mine, :],
                    send_sem=send_sem,
                    recv_sem=recv_sem,
                    device_id={"head": place},
                    device_id_type=MESH,
                ).start()
            return carry

        lax.fori_loop(0, n - 1, body, 0)

    def send_head(head):
        scatter(
            head,
            ((k_ref, kvbuf.at[head, 0]), (v_ref, kvbuf.at[head, 1])),
            kv_send.at[head],
            kv_recv.at[head],
        )
        scatter(head, ((q_ref, qbuf.at[head]),), q_send.at[head], q_recv.at[head])

    def wait_sent(head):
        sent = pl.ds(0, (n - 1) * tokens)
        kv = kvbuf.at[head, :, sent, :]
        pltpu.make_async_copy(kv, kv, kv_send.at[head]).wait()
        q = qbuf.at[head, sent, :]
        pltpu.make_async_copy(q, q, q_send.at[head]).wait()

    def hand_on(head, slot):
        return pltpu.make_async_remote_copy(
            src_ref=kvbuf.at[head] if slot == 0 else slots.at[slot - 1, head],
            dst_ref=slots.at[slot, head],
            send_sem=slot_send.at[slot, head],
            recv_sem=slot_recv.at[slot, head],
            device_id={"group": group + 1},
            device_id_type=MESH,
        )

    def compute(head):
        head_number = me * heads + head
        first_key = kvbuf[head, 0, 0:16, :].astype(jnp.float32)[0:1, :]
        positions = lax.broadcasted_iota(jnp.int32, (seq, HD), 0)
        for offset in range(WIN):
            source = jnp.maximum(group - offset, 0)
            live = jnp.where(
                group >= offset, count_ref[source] * mask_ref[group, source, head_number], 0
            )
            valid = positions < live
            block = kvbuf.at[head] if offset == 0 else slots.at[offset - 1, head]
            rows = pl.ds(offset * seq, seq)
            kall[rows, :] = jnp.where(
                valid, block[0].astype(jnp.float32), first_key
            ).astype(jnp.bfloat16)
            vall[rows, 0:HD] = jnp.where(valid, block[1].astype(jnp.float32), 0.0).astype(
                jnp.bfloat16
            )
            vall[rows, HD : 2 * HD] = jnp.where(valid, 1.0, 0.0).astype(jnp.bfloat16)
        gates = gate_ref[:, columns(me, head)]
        levels = lax.broadcasted_iota(jnp.int32, gates.shape, 0)
        gate = jnp.sum(
            jnp.where(levels == level_ref[group], gates, 0.0), axis=0, keepdims=True
        )

        def body(step, carry):
            index = lax.rem(step + me // per + n_tiles // 2, n_tiles)
            start = pl.multiple_of(index * tile, tile)
            scores = lax.dot_general(
                qbuf[head, pl.ds(start, tile), :],
                kall[...],
                (((1,), (1,)), ((), ())),
                preferred_element_type=jnp.float32,
            )
            top = jnp.max(scores, axis=1, keepdims=True)
            weights = jnp.exp2((scores - top) * scale).astype(jnp.bfloat16)
            summed = jnp.dot(weights, vall[...], preferred_element_type=jnp.float32)
            gated = summed[:, 0:HD] / summed[:, HD : 2 * HD] * gate
            obuf[head, pl.ds(start, tile), :] = gated.astype(jnp.bfloat16)
            for piece in range(per):
                place = index * per + piece
                piece_rows = pl.ds(pl.multiple_of(place * tokens, tokens), tokens)
                finished = obuf.at[head, piece_rows, :]
                landing = out_ref.at[0, :, columns(me, head)]

                @pl.when(place == me)
                def _():
                    pltpu.make_async_copy(finished, landing, out_recv).start()

                @pl.when(place != me)
                def _():
                    pltpu.make_async_remote_copy(
                        src_ref=finished,
                        dst_ref=landing,
                        send_sem=out_send,
                        recv_sem=out_recv,
                        device_id={"head": place},
                        device_id_type=MESH,
                    ).start()

            return carry

        lax.fori_loop(0, n_tiles, body, 0)

    for head in range(min(AHEAD, heads)):
        send_head(head)
    for stage in range(heads + 1):
        if stage < heads:
            pltpu.make_async_copy(kvbuf.at[stage], kvbuf.at[stage], kv_recv.at[stage]).wait()

            @pl.when(has_next)
            def _():
                hand_on(stage, 0).start()

            if stage + AHEAD < heads:
                wait_sent(stage)
                send_head(stage + AHEAD)

            @pl.when(group >= 1)
            def _():
                hand_on(stage, 0).wait_recv()

                @pl.when(has_next)
                def _():
                    hand_on(stage, 1).start()

        if stage >= 1:
            head = stage - 1
            pltpu.make_async_copy(qbuf.at[head], qbuf.at[head], q_recv.at[head]).wait()

            @pl.when(group >= 2)
            def _():
                hand_on(head, 1).wait_recv()

            compute(head)

    for head in range(heads):
        if head + AHEAD >= heads:
            wait_sent(head)

        @pl.when(has_next)
        def _():
            hand_on(head, 0).wait_send()

            @pl.when(group >= 1)
            def _():
                hand_on(head, 1).wait_send()

    sent = obuf.at[:, pl.ds(0, (n - 1) * tokens), :]
    pltpu.make_async_copy(sent, sent, out_send).wait()
    pltpu.make_async_copy(out_ref, out_ref, out_recv).wait()


def solution(mesh):
    n = mesh.shape["head"]
    groups = mesh.shape["group"]

    def shards(queries, keys, values, group_mask, noise_level, token_count, level_gate):
        _, tokens, features = queries.shape
        heads = features // HD // n
        seq = tokens * n
        tile = max(tokens, 256 if seq <= 1024 else 128)
        any_space = pl.BlockSpec(memory_space=pl.ANY)
        smem = pl.BlockSpec(memory_space=pltpu.SMEM)
        dma = pltpu.SemaphoreType.DMA
        scores = heads * seq * seq * WIN
        return pl.pallas_call(
            functools.partial(kernel, n, groups, tile),
            out_shape=jax.ShapeDtypeStruct(queries.shape, jnp.bfloat16),
            in_specs=[any_space] * 3 + [smem] * 3 + [pl.BlockSpec(memory_space=pltpu.VMEM)],
            out_specs=any_space,
            scratch_shapes=[
                pltpu.VMEM((heads, seq, HD), jnp.bfloat16),
                pltpu.VMEM((heads, 2, seq, HD), jnp.bfloat16),
                pltpu.VMEM((WIN - 1, heads, 2, seq, HD), jnp.bfloat16),
                pltpu.VMEM((WIN * seq, HD), jnp.bfloat16),
                pltpu.VMEM((WIN * seq, 2 * HD), jnp.bfloat16),
                pltpu.VMEM((heads, seq, HD), jnp.bfloat16),
                dma((heads,)),
                dma((heads,)),
                dma((heads,)),
                dma((heads,)),
                dma((WIN - 1, heads)),
                dma((WIN - 1, heads)),
                dma,
                dma,
            ],
            compiler_params=pltpu.CompilerParams(
                collective_id=0, has_side_effects=True, vmem_limit_bytes=56 * 1024 * 1024
            ),
            cost_estimate=pl.CostEstimate(
                flops=scores * HD * 4, bytes_accessed=queries.size * 8, transcendentals=scores
            ),
        )(queries, keys, values, group_mask, noise_level, token_count, level_gate)

    return jax.shard_map(
        shards,
        mesh=mesh,
        in_specs=(P("group", "head", None),) * 3 + (P(),) * 4,
        out_specs=P("group", "head", None),
        check_vma=False,
    )
```

```python
import functools
import math

import jax
import jax.numpy as jnp
from jax import lax
from jax.experimental import pallas as pl
from jax.experimental.pallas import tpu as pltpu
from jax.sharding import PartitionSpec as P

HD = 128
WIN = 3
AHEAD = 4
MESH = pl.DeviceIdType.MESH


def kernel(
    n, groups, tile,
    q_ref, k_ref, v_ref, mask_ref, level_ref, count_ref, gate_ref, out_ref,
    qbuf, kvbuf, slots, kall, vall, obuf,
    kv_send, kv_recv, q_send, q_recv, slot_send, slot_recv, out_send, out_recv,
):
    group = lax.axis_index("group")
    me = lax.axis_index("head")
    heads, seq, _ = qbuf.shape
    tokens = seq // n
    half = n // 2
    has_next = group < groups - 1
    per = tile // tokens
    n_tiles = seq // tile
    scale = HD ** -0.5 * math.log2(math.e)
    mine = pl.ds(pl.multiple_of(me * tokens, tokens), tokens)

    def columns(place, head):
        return pl.ds(pl.multiple_of((place * heads + head) * HD, HD), HD)

    barrier = pltpu.get_barrier_semaphore()

    def greet(step, carry):
        pl.semaphore_signal(
            barrier, inc=1, device_id={"head": lax.rem(me + step, n)}, device_id_type=MESH
        )
        return carry

    lax.fori_loop(1, n, greet, 0)

    @pl.when(has_next)
    def _():
        pl.semaphore_signal(barrier, inc=1, device_id={"group": group + 1}, device_id_type=MESH)

    @pl.when(group >= 1)
    def _():
        pl.semaphore_signal(barrier, inc=1, device_id={"group": group - 1}, device_id_type=MESH)

    beside = jnp.minimum(group, 1) + jnp.minimum(groups - 1 - group, 1)
    pl.semaphore_wait(barrier, n - 1 + beside)

    def scatter(head, pairs, send_sem, recv_sem):
        for source, target in pairs:
            pltpu.make_async_copy(
                source.at[0, :, columns(me, head)], target.at[mine, :], recv_sem
            ).start()

        def body(step, carry):
            odd = step % 2
            shift = odd * ((step + 1) // 2) + (1 - odd) * (half + step // 2)
            place = lax.rem(me + shift, n)
            for source, target in pairs:
                pltpu.make_async_remote_copy(
                    src_ref=source.at[0, :, columns(place, head)],
                    dst_ref=target.at[mine, :],
                    send_sem=send_sem,
                    recv_sem=recv_sem,
                    device_id={"head": place},
                    device_id_type=MESH,
                ).start()
            return carry

        lax.fori_loop(0, n - 1, body, 0)

    def send_head(head):
        scatter(
            head,
            ((k_ref, kvbuf.at[head, 0]), (v_ref, kvbuf.at[head, 1])),
            kv_send.at[head],
            kv_recv.at[head],
        )
        scatter(head, ((q_ref, qbuf.at[head]),), q_send.at[head], q_recv.at[head])

    def wait_sent(head):
        sent = pl.ds(0, (n - 1) * tokens)
        kv = kvbuf.at[head, :, sent, :]
        pltpu.make_async_copy(kv, kv, kv_send.at[head]).wait()
        q = qbuf.at[head, sent, :]
        pltpu.make_async_copy(q, q, q_send.at[head]).wait()

    def hand_on(head, slot):
        return pltpu.make_async_remote_copy(
            src_ref=kvbuf.at[head] if slot == 0 else slots.at[slot - 1, head],
            dst_ref=slots.at[slot, head],
            send_sem=slot_send.at[slot, head],
            recv_sem=slot_recv.at[slot, head],
            device_id={"group": group + 1},
            device_id_type=MESH,
        )

    def prepare(head):
        head_number = me * heads + head
        first_key = kvbuf[head, 0, 0:16, :].astype(jnp.float32)[0:1, :]
        positions = lax.broadcasted_iota(jnp.int32, (seq, HD), 0)
        for offset in range(WIN):
            source = jnp.maximum(group - offset, 0)
            live = jnp.where(
                group >= offset, count_ref[source] * mask_ref[group, source, head_number], 0
            )
            valid = positions < live
            block = kvbuf.at[head] if offset == 0 else slots.at[offset - 1, head]
            rows = pl.ds(offset * seq, seq)
            kall[rows, :] = jnp.where(
                valid, block[0].astype(jnp.float32), first_key
            ).astype(jnp.bfloat16)
            vall[rows, 0:HD] = jnp.where(valid, block[1].astype(jnp.float32), 0.0).astype(
                jnp.bfloat16
            )
            vall[rows, HD : 2 * HD] = jnp.where(valid, 1.0, 0.0).astype(jnp.bfloat16)

    def attend(head, first, last):
        gates = gate_ref[:, columns(me, head)]
        levels = lax.broadcasted_iota(jnp.int32, gates.shape, 0)
        gate = jnp.sum(
            jnp.where(levels == level_ref[group], gates, 0.0), axis=0, keepdims=True
        )

        def body(step, carry):
            index = lax.rem(step + me // per + n_tiles // 2, n_tiles)
            start = pl.multiple_of(index * tile, tile)
            rows = qbuf[head, pl.ds(start, tile), :]
            tops, sums = [], []
            for offset in range(WIN):
                keys = pl.ds(offset * seq, seq)
                scores = lax.dot_general(
                    rows, kall[keys, :], (((1,), (1,)), ((), ())),
                    preferred_element_type=jnp.float32,
                )
                top = jnp.max(scores, axis=1, keepdims=True)
                weights = jnp.exp2((scores - top) * scale).astype(jnp.bfloat16)
                tops.append(top)
                sums.append(jnp.dot(weights, vall[keys, :], preferred_element_type=jnp.float32))
            joint = functools.reduce(jnp.maximum, tops)
            summed = sum(
                jnp.exp2((top - joint) * scale) * part for top, part in zip(tops, sums)
            )
            gated = summed[:, 0:HD] / summed[:, HD : 2 * HD] * gate
            obuf[head, pl.ds(start, tile), :] = gated.astype(jnp.bfloat16)
            for piece in range(per):
                place = index * per + piece
                piece_rows = pl.ds(pl.multiple_of(place * tokens, tokens), tokens)
                finished = obuf.at[head, piece_rows, :]
                landing = out_ref.at[0, :, columns(me, head)]

                @pl.when(place == me)
                def _():
                    pltpu.make_async_copy(finished, landing, out_recv).start()

                @pl.when(place != me)
                def _():
                    pltpu.make_async_remote_copy(
                        src_ref=finished,
                        dst_ref=landing,
                        send_sem=out_send,
                        recv_sem=out_recv,
                        device_id={"head": place},
                        device_id_type=MESH,
                    ).start()

            return carry

        lax.fori_loop(first, last, body, 0)

    for head in range(min(AHEAD, heads)):
        send_head(head)
    for stage in range(heads + 1):
        head = stage - 1
        if stage < heads:
            pltpu.make_async_copy(kvbuf.at[stage], kvbuf.at[stage], kv_recv.at[stage]).wait()

            @pl.when(has_next)
            def _():
                hand_on(stage, 0).start()

            if stage + AHEAD < heads:
                wait_sent(stage)
                send_head(stage + AHEAD)

        if stage >= 1:
            pltpu.make_async_copy(qbuf.at[head], qbuf.at[head], q_recv.at[head]).wait()

            @pl.when(group >= 2)
            def _():
                hand_on(head, 1).wait_recv()

            prepare(head)
            attend(head, 0, n_tiles // 2)

        if stage < heads:

            @pl.when(group >= 1)
            def _():
                hand_on(stage, 0).wait_recv()

                @pl.when(has_next)
                def _():
                    hand_on(stage, 1).start()

        if stage >= 1:
            attend(head, n_tiles // 2, n_tiles)

    for head in range(heads):
        if head + AHEAD >= heads:
            wait_sent(head)

        @pl.when(has_next)
        def _():
            hand_on(head, 0).wait_send()

            @pl.when(group >= 1)
            def _():
                hand_on(head, 1).wait_send()

    sent = obuf.at[:, pl.ds(0, (n - 1) * tokens), :]
    pltpu.make_async_copy(sent, sent, out_send).wait()
    pltpu.make_async_copy(out_ref, out_ref, out_recv).wait()


def solution(mesh):
    n = mesh.shape["head"]
    groups = mesh.shape["group"]

    def shards(queries, keys, values, group_mask, noise_level, token_count, level_gate):
        _, tokens, features = queries.shape
        heads = features // HD // n
        seq = tokens * n
        tile = max(tokens, 256 if seq <= 1024 else 128)
        any_space = pl.BlockSpec(memory_space=pl.ANY)
        smem = pl.BlockSpec(memory_space=pltpu.SMEM)
        dma = pltpu.SemaphoreType.DMA
        scores = heads * seq * seq * WIN
        return pl.pallas_call(
            functools.partial(kernel, n, groups, tile),
            out_shape=jax.ShapeDtypeStruct(queries.shape, jnp.bfloat16),
            in_specs=[any_space] * 3 + [smem] * 3 + [pl.BlockSpec(memory_space=pltpu.VMEM)],
            out_specs=any_space,
            scratch_shapes=[
                pltpu.VMEM((heads, seq, HD), jnp.bfloat16),
                pltpu.VMEM((heads, 2, seq, HD), jnp.bfloat16),
                pltpu.VMEM((WIN - 1, heads, 2, seq, HD), jnp.bfloat16),
                pltpu.VMEM((WIN * seq, HD), jnp.bfloat16),
                pltpu.VMEM((WIN * seq, 2 * HD), jnp.bfloat16),
                pltpu.VMEM((heads, seq, HD), jnp.bfloat16),
                dma((heads,)),
                dma((heads,)),
                dma((heads,)),
                dma((heads,)),
                dma((WIN - 1, heads)),
                dma((WIN - 1, heads)),
                dma,
                dma,
            ],
            compiler_params=pltpu.CompilerParams(
                collective_id=0, has_side_effects=True, vmem_limit_bytes=56 * 1024 * 1024
            ),
            cost_estimate=pl.CostEstimate(
                flops=scores * HD * 4, bytes_accessed=queries.size * 8, transcendentals=scores
            ),
        )(queries, keys, values, group_mask, noise_level, token_count, level_gate)

    return jax.shard_map(
        shards,
        mesh=mesh,
        in_specs=(P("group", "head", None),) * 3 + (P(),) * 4,
        out_specs=P("group", "head", None),
        check_vma=False,
    )
```

```python
import functools
import math

import jax
import jax.numpy as jnp
from jax import lax
from jax.experimental import pallas as pl
from jax.experimental.pallas import tpu as pltpu
from jax.sharding import PartitionSpec as P

HD = 128
WIN = 3
MESH = pl.DeviceIdType.MESH


def kernel(
    n, groups, tile,
    q_ref, k_ref, v_ref, mask_ref, level_ref, count_ref, gate_ref, out_ref,
    qbuf, kvbuf, slots, kall, vall, obuf,
    kv_send, kv_recv, q_send, q_recv, slot_send, slot_recv, out_send, out_recv,
):
    group = lax.axis_index("group")
    me = lax.axis_index("head")
    heads, seq, _ = qbuf.shape
    tokens = seq // n
    half = n // 2
    has_next = group < groups - 1
    per = tile // tokens
    n_tiles = seq // tile
    scale = HD ** -0.5 * math.log2(math.e)
    mine = pl.ds(pl.multiple_of(me * tokens, tokens), tokens)

    def columns(place, head):
        return pl.ds(pl.multiple_of((place * heads + head) * HD, HD), HD)

    barrier = pltpu.get_barrier_semaphore()

    def greet(step, carry):
        pl.semaphore_signal(
            barrier, inc=1, device_id={"head": lax.rem(me + step, n)}, device_id_type=MESH
        )
        return carry

    lax.fori_loop(1, n, greet, 0)

    @pl.when(has_next)
    def _():
        pl.semaphore_signal(barrier, inc=1, device_id={"group": group + 1}, device_id_type=MESH)

    @pl.when(group >= 1)
    def _():
        pl.semaphore_signal(barrier, inc=1, device_id={"group": group - 1}, device_id_type=MESH)

    beside = jnp.minimum(group, 1) + jnp.minimum(groups - 1 - group, 1)
    pl.semaphore_wait(barrier, n - 1 + beside)

    def scatter(head, pairs, send_sem, recv_sem):
        for source, target in pairs:
            pltpu.make_async_copy(
                source.at[0, :, columns(me, head)], target.at[mine, :], recv_sem
            ).start()

        def body(step, carry):
            odd = step % 2
            shift = odd * ((step + 1) // 2) + (1 - odd) * (half + step // 2)
            place = lax.rem(me + shift, n)
            for source, target in pairs:
                pltpu.make_async_remote_copy(
                    src_ref=source.at[0, :, columns(place, head)],
                    dst_ref=target.at[mine, :],
                    send_sem=send_sem,
                    recv_sem=recv_sem,
                    device_id={"head": place},
                    device_id_type=MESH,
                ).start()
            return carry

        lax.fori_loop(0, n - 1, body, 0)

    def send_keys(head):
        scatter(
            head,
            ((k_ref, kvbuf.at[head, 0]), (v_ref, kvbuf.at[head, 1])),
            kv_send.at[head],
            kv_recv.at[head],
        )

    def send_queries(head):
        scatter(head, ((q_ref, qbuf.at[head]),), q_send.at[head], q_recv.at[head])

    def wait_sent(head):
        sent = pl.ds(0, (n - 1) * tokens)
        kv = kvbuf.at[head, :, sent, :]
        pltpu.make_async_copy(kv, kv, kv_send.at[head]).wait()
        q = qbuf.at[head, sent, :]
        pltpu.make_async_copy(q, q, q_send.at[head]).wait()

    def hand_on(head, slot):
        return pltpu.make_async_remote_copy(
            src_ref=kvbuf.at[head] if slot == 0 else slots.at[slot - 1, head],
            dst_ref=slots.at[slot, head],
            send_sem=slot_send.at[slot, head],
            recv_sem=slot_recv.at[slot, head],
            device_id={"group": group + 1},
            device_id_type=MESH,
        )

    def prepare(head):
        head_number = me * heads + head
        first_key = kvbuf[head, 0, 0:16, :].astype(jnp.float32)[0:1, :]
        positions = lax.broadcasted_iota(jnp.int32, (seq, HD), 0)
        for offset in range(WIN):
            source = jnp.maximum(group - offset, 0)
            live = jnp.where(
                group >= offset, count_ref[source] * mask_ref[group, source, head_number], 0
            )
            valid = positions < live
            block = kvbuf.at[head] if offset == 0 else slots.at[offset - 1, head]
            rows = pl.ds(offset * seq, seq)
            kall[rows, :] = jnp.where(
                valid, block[0].astype(jnp.float32), first_key
            ).astype(jnp.bfloat16)
            vall[rows, 0:HD] = jnp.where(valid, block[1].astype(jnp.float32), 0.0).astype(
                jnp.bfloat16
            )
            vall[rows, HD : 2 * HD] = jnp.where(valid, 1.0, 0.0).astype(jnp.bfloat16)

    def attend(head, first, last):
        gates = gate_ref[:, columns(me, head)]
        levels = lax.broadcasted_iota(jnp.int32, gates.shape, 0)
        gate = jnp.sum(
            jnp.where(levels == level_ref[group], gates, 0.0), axis=0, keepdims=True
        )

        def body(step, carry):
            index = lax.rem(step + me // per + n_tiles // 2, n_tiles)
            start = pl.multiple_of(index * tile, tile)
            rows = qbuf[head, pl.ds(start, tile), :]
            tops, sums = [], []
            for offset in range(WIN):
                keys = pl.ds(offset * seq, seq)
                scores = lax.dot_general(
                    rows, kall[keys, :], (((1,), (1,)), ((), ())),
                    preferred_element_type=jnp.float32,
                )
                top = jnp.max(scores, axis=1, keepdims=True)
                weights = jnp.exp2((scores - top) * scale).astype(jnp.bfloat16)
                tops.append(top)
                sums.append(jnp.dot(weights, vall[keys, :], preferred_element_type=jnp.float32))
            joint = functools.reduce(jnp.maximum, tops)
            summed = sum(
                jnp.exp2((top - joint) * scale) * part for top, part in zip(tops, sums)
            )
            gated = summed[:, 0:HD] / summed[:, HD : 2 * HD] * gate
            obuf[head, pl.ds(start, tile), :] = gated.astype(jnp.bfloat16)
            for piece in range(per):
                place = index * per + piece
                piece_rows = pl.ds(pl.multiple_of(place * tokens, tokens), tokens)
                finished = obuf.at[head, piece_rows, :]
                landing = out_ref.at[0, :, columns(me, head)]

                @pl.when(place == me)
                def _():
                    pltpu.make_async_copy(finished, landing, out_recv).start()

                @pl.when(place != me)
                def _():
                    pltpu.make_async_remote_copy(
                        src_ref=finished,
                        dst_ref=landing,
                        send_sem=out_send,
                        recv_sem=out_recv,
                        device_id={"head": place},
                        device_id_type=MESH,
                    ).start()

            return carry

        lax.fori_loop(first, last, body, 0)

    send_keys(0)
    for head in range(heads):
        if head + 1 < heads:
            send_keys(head + 1)
        send_queries(head)
    for stage in range(heads + 1):
        head = stage - 1
        if stage < heads:
            pltpu.make_async_copy(kvbuf.at[stage], kvbuf.at[stage], kv_recv.at[stage]).wait()

            @pl.when(has_next)
            def _():
                hand_on(stage, 0).start()

        if stage >= 1:
            pltpu.make_async_copy(qbuf.at[head], qbuf.at[head], q_recv.at[head]).wait()

            @pl.when(group >= 2)
            def _():
                hand_on(head, 1).wait_recv()

            prepare(head)
            attend(head, 0, n_tiles // 2)

        if stage < heads:

            @pl.when(group >= 1)
            def _():
                hand_on(stage, 0).wait_recv()

                @pl.when(has_next)
                def _():
                    hand_on(stage, 1).start()

        if stage >= 1:
            attend(head, n_tiles // 2, n_tiles)

    for head in range(heads):
        wait_sent(head)

        @pl.when(has_next)
        def _():
            hand_on(head, 0).wait_send()

            @pl.when(group >= 1)
            def _():
                hand_on(head, 1).wait_send()

    sent = obuf.at[:, pl.ds(0, (n - 1) * tokens), :]
    pltpu.make_async_copy(sent, sent, out_send).wait()
    pltpu.make_async_copy(out_ref, out_ref, out_recv).wait()


def solution(mesh):
    n = mesh.shape["head"]
    groups = mesh.shape["group"]

    def shards(queries, keys, values, group_mask, noise_level, token_count, level_gate):
        _, tokens, features = queries.shape
        heads = features // HD // n
        seq = tokens * n
        tile = max(tokens, 256 if seq <= 1024 else 128)
        any_space = pl.BlockSpec(memory_space=pl.ANY)
        smem = pl.BlockSpec(memory_space=pltpu.SMEM)
        dma = pltpu.SemaphoreType.DMA
        scores = heads * seq * seq * WIN
        return pl.pallas_call(
            functools.partial(kernel, n, groups, tile),
            out_shape=jax.ShapeDtypeStruct(queries.shape, jnp.bfloat16),
            in_specs=[any_space] * 3 + [smem] * 3 + [pl.BlockSpec(memory_space=pltpu.VMEM)],
            out_specs=any_space,
            scratch_shapes=[
                pltpu.VMEM((heads, seq, HD), jnp.bfloat16),
                pltpu.VMEM((heads, 2, seq, HD), jnp.bfloat16),
                pltpu.VMEM((WIN - 1, heads, 2, seq, HD), jnp.bfloat16),
                pltpu.VMEM((WIN * seq, HD), jnp.bfloat16),
                pltpu.VMEM((WIN * seq, 2 * HD), jnp.bfloat16),
                pltpu.VMEM((heads, seq, HD), jnp.bfloat16),
                dma((heads,)),
                dma((heads,)),
                dma((heads,)),
                dma((heads,)),
                dma((WIN - 1, heads)),
                dma((WIN - 1, heads)),
                dma,
                dma,
            ],
            compiler_params=pltpu.CompilerParams(
                collective_id=0, has_side_effects=True, vmem_limit_bytes=56 * 1024 * 1024
            ),
            cost_estimate=pl.CostEstimate(
                flops=scores * HD * 4, bytes_accessed=queries.size * 8, transcendentals=scores
            ),
        )(queries, keys, values, group_mask, noise_level, token_count, level_gate)

    return jax.shard_map(
        shards,
        mesh=mesh,
        in_specs=(P("group", "head", None),) * 3 + (P(),) * 4,
        out_specs=P("group", "head", None),
        check_vma=False,
    )
```

```python
import functools
import math

import jax
import jax.numpy as jnp
from jax import lax
from jax.experimental import pallas as pl
from jax.experimental.pallas import tpu as pltpu
from jax.sharding import PartitionSpec as P

HD = 128
WIN = 3
MESH = pl.DeviceIdType.MESH


def kernel(
    n, groups, tile,
    q_ref, k_ref, v_ref, mask_ref, level_ref, count_ref, gate_ref, out_ref,
    qbuf, kvbuf, slots, kall, vall, obuf,
    kv_send, kv_recv, q_send, q_recv, slot_send, slot_recv, out_send, out_recv,
):
    group = lax.axis_index("group")
    me = lax.axis_index("head")
    heads, seq, _ = qbuf.shape
    tokens = seq // n
    half = n // 2
    has_next = group < groups - 1
    per = tile // tokens
    n_tiles = seq // tile
    scale = HD ** -0.5 * math.log2(math.e)
    mine = pl.ds(pl.multiple_of(me * tokens, tokens), tokens)

    def columns(place, head):
        return pl.ds(pl.multiple_of((place * heads + head) * HD, HD), HD)

    barrier = pltpu.get_barrier_semaphore()

    def greet(step, carry):
        pl.semaphore_signal(
            barrier, inc=1, device_id={"head": lax.rem(me + step, n)}, device_id_type=MESH
        )
        return carry

    lax.fori_loop(1, n, greet, 0)

    @pl.when(has_next)
    def _():
        pl.semaphore_signal(barrier, inc=1, device_id={"group": group + 1}, device_id_type=MESH)

    @pl.when(group >= 1)
    def _():
        pl.semaphore_signal(barrier, inc=1, device_id={"group": group - 1}, device_id_type=MESH)

    beside = jnp.minimum(group, 1) + jnp.minimum(groups - 1 - group, 1)
    pl.semaphore_wait(barrier, n - 1 + beside)

    def scatter(head, pairs, send_sem, recv_sem):
        for source, target in pairs:
            pltpu.make_async_copy(
                source.at[0, :, columns(me, head)], target.at[mine, :], recv_sem
            ).start()

        def body(step, carry):
            odd = step % 2
            shift = odd * ((step + 1) // 2) + (1 - odd) * (half + step // 2)
            place = lax.rem(me + shift, n)
            for source, target in pairs:
                pltpu.make_async_remote_copy(
                    src_ref=source.at[0, :, columns(place, head)],
                    dst_ref=target.at[mine, :],
                    send_sem=send_sem,
                    recv_sem=recv_sem,
                    device_id={"head": place},
                    device_id_type=MESH,
                ).start()
            return carry

        lax.fori_loop(0, n - 1, body, 0)

    def send_keys(head):
        scatter(
            head,
            ((k_ref, kvbuf.at[head, 0]), (v_ref, kvbuf.at[head, 1])),
            kv_send.at[head],
            kv_recv.at[head],
        )

    def send_queries(head):
        scatter(head, ((q_ref, qbuf.at[head]),), q_send.at[head], q_recv.at[head])

    def wait_sent(head):
        sent = pl.ds(0, (n - 1) * tokens)
        kv = kvbuf.at[head, :, sent, :]
        pltpu.make_async_copy(kv, kv, kv_send.at[head]).wait()
        q = qbuf.at[head, sent, :]
        pltpu.make_async_copy(q, q, q_send.at[head]).wait()

    def hand_on(head, slot):
        return pltpu.make_async_remote_copy(
            src_ref=kvbuf.at[head] if slot == 0 else slots.at[slot - 1, head],
            dst_ref=slots.at[slot, head],
            send_sem=slot_send.at[slot, head],
            recv_sem=slot_recv.at[slot, head],
            device_id={"group": group + 1},
            device_id_type=MESH,
        )

    def prepare(head):
        head_number = me * heads + head
        first_key = kvbuf[head, 0, 0:16, :].astype(jnp.float32)[0:1, :]
        positions = lax.broadcasted_iota(jnp.int32, (seq, HD), 0)
        for offset in range(WIN):
            source = jnp.maximum(group - offset, 0)
            live = jnp.where(
                group >= offset, count_ref[source] * mask_ref[group, source, head_number], 0
            )
            valid = positions < live
            block = kvbuf.at[head] if offset == 0 else slots.at[offset - 1, head]
            rows = pl.ds(offset * seq, seq)
            kall[rows, :] = jnp.where(
                valid, block[0].astype(jnp.float32), first_key
            ).astype(jnp.bfloat16)
            vall[rows, 0:HD] = jnp.where(valid, block[1].astype(jnp.float32), 0.0).astype(
                jnp.bfloat16
            )
            vall[rows, HD : 2 * HD] = jnp.where(valid, 1.0, 0.0).astype(jnp.bfloat16)

    def held_back(head):
        return head + 2 < heads

    def send_result(head, place):
        rows = pl.ds(pl.multiple_of(place * tokens, tokens), tokens)
        finished = obuf.at[head, rows, :]
        landing = out_ref.at[0, :, columns(me, head)]

        @pl.when(place == me)
        def _():
            pltpu.make_async_copy(finished, landing, out_recv).start()

        @pl.when(place != me)
        def _():
            pltpu.make_async_remote_copy(
                src_ref=finished,
                dst_ref=landing,
                send_sem=out_send,
                recv_sem=out_recv,
                device_id={"head": place},
                device_id_type=MESH,
            ).start()

    def attend(head, first, last):
        gates = gate_ref[:, columns(me, head)]
        levels = lax.broadcasted_iota(jnp.int32, gates.shape, 0)
        gate = jnp.sum(
            jnp.where(levels == level_ref[group], gates, 0.0), axis=0, keepdims=True
        )

        def body(step, carry):
            index = lax.rem(step + me // per + n_tiles // 2, n_tiles)
            start = pl.multiple_of(index * tile, tile)
            rows = qbuf[head, pl.ds(start, tile), :]
            tops, sums = [], []
            for offset in range(WIN):
                keys = pl.ds(offset * seq, seq)
                scores = lax.dot_general(
                    rows, kall[keys, :], (((1,), (1,)), ((), ())),
                    preferred_element_type=jnp.float32,
                )
                top = jnp.max(scores, axis=1, keepdims=True)
                weights = jnp.exp2((scores - top) * scale).astype(jnp.bfloat16)
                tops.append(top)
                sums.append(jnp.dot(weights, vall[keys, :], preferred_element_type=jnp.float32))
            joint = functools.reduce(jnp.maximum, tops)
            summed = sum(
                jnp.exp2((top - joint) * scale) * part for top, part in zip(tops, sums)
            )
            gated = summed[:, 0:HD] / summed[:, HD : 2 * HD] * gate
            obuf[head, pl.ds(start, tile), :] = gated.astype(jnp.bfloat16)
            if not held_back(head):
                for piece in range(per):
                    send_result(head, index * per + piece)
            return carry

        lax.fori_loop(first, last, body, 0)

    send_keys(0)
    for head in range(heads):
        if head + 1 < heads:
            send_keys(head + 1)
        send_queries(head)
    for stage in range(heads + 1):
        head = stage - 1
        if stage < heads:
            pltpu.make_async_copy(kvbuf.at[stage], kvbuf.at[stage], kv_recv.at[stage]).wait()

            @pl.when(has_next)
            def _():
                hand_on(stage, 0).start()

        if stage >= 1:
            pltpu.make_async_copy(qbuf.at[head], qbuf.at[head], q_recv.at[head]).wait()

            @pl.when(group >= 2)
            def _():
                hand_on(head, 1).wait_recv()

            prepare(head)
            attend(head, 0, n_tiles // 2)

        if stage < heads:

            @pl.when(group >= 1)
            def _():
                hand_on(stage, 0).wait_recv()

                @pl.when(has_next)
                def _():
                    hand_on(stage, 1).start()

        if stage >= 1:
            attend(head, n_tiles // 2, n_tiles)

        if stage == heads - 1:
            for early in range(heads):
                if held_back(early):

                    def body(step, carry):
                        send_result(early, lax.rem(me + half + step, n))
                        return carry

                    lax.fori_loop(0, n, body, 0)

    for head in range(heads):
        wait_sent(head)

        @pl.when(has_next)
        def _():
            hand_on(head, 0).wait_send()

            @pl.when(group >= 1)
            def _():
                hand_on(head, 1).wait_send()

    sent = obuf.at[:, pl.ds(0, (n - 1) * tokens), :]
    pltpu.make_async_copy(sent, sent, out_send).wait()
    pltpu.make_async_copy(out_ref, out_ref, out_recv).wait()


def solution(mesh):
    n = mesh.shape["head"]
    groups = mesh.shape["group"]

    def shards(queries, keys, values, group_mask, noise_level, token_count, level_gate):
        _, tokens, features = queries.shape
        heads = features // HD // n
        seq = tokens * n
        tile = max(tokens, 256 if seq <= 1024 else 128)
        any_space = pl.BlockSpec(memory_space=pl.ANY)
        smem = pl.BlockSpec(memory_space=pltpu.SMEM)
        dma = pltpu.SemaphoreType.DMA
        scores = heads * seq * seq * WIN
        return pl.pallas_call(
            functools.partial(kernel, n, groups, tile),
            out_shape=jax.ShapeDtypeStruct(queries.shape, jnp.bfloat16),
            in_specs=[any_space] * 3 + [smem] * 3 + [pl.BlockSpec(memory_space=pltpu.VMEM)],
            out_specs=any_space,
            scratch_shapes=[
                pltpu.VMEM((heads, seq, HD), jnp.bfloat16),
                pltpu.VMEM((heads, 2, seq, HD), jnp.bfloat16),
                pltpu.VMEM((WIN - 1, heads, 2, seq, HD), jnp.bfloat16),
                pltpu.VMEM((WIN * seq, HD), jnp.bfloat16),
                pltpu.VMEM((WIN * seq, 2 * HD), jnp.bfloat16),
                pltpu.VMEM((heads, seq, HD), jnp.bfloat16),
                dma((heads,)),
                dma((heads,)),
                dma((heads,)),
                dma((heads,)),
                dma((WIN - 1, heads)),
                dma((WIN - 1, heads)),
                dma,
                dma,
            ],
            compiler_params=pltpu.CompilerParams(
                collective_id=0, has_side_effects=True, vmem_limit_bytes=56 * 1024 * 1024
            ),
            cost_estimate=pl.CostEstimate(
                flops=scores * HD * 4, bytes_accessed=queries.size * 8, transcendentals=scores
            ),
        )(queries, keys, values, group_mask, noise_level, token_count, level_gate)

    return jax.shard_map(
        shards,
        mesh=mesh,
        in_specs=(P("group", "head", None),) * 3 + (P(),) * 4,
        out_specs=P("group", "head", None),
        check_vma=False,
    )
```

```python
import functools
import math

import jax
import jax.numpy as jnp
from jax import lax
from jax.experimental import pallas as pl
from jax.experimental.pallas import tpu as pltpu
from jax.sharding import PartitionSpec as P

HD = 128
WIN = 3
MESH = pl.DeviceIdType.MESH


def kernel(
    n, groups, tile,
    q_ref, k_ref, v_ref, mask_ref, level_ref, count_ref, gate_ref, out_ref,
    qbuf, kvbuf, slots, kall, vall, obuf,
    kv_send, kv_recv, q_send, q_recv, slot_send, slot_recv, out_send, out_recv,
):
    group = lax.axis_index("group")
    me = lax.axis_index("head")
    heads, seq, _ = qbuf.shape
    tokens = seq // n
    half = n // 2
    has_next = group < groups - 1
    per = tile // tokens
    n_tiles = seq // tile
    scale = HD ** -0.5 * math.log2(math.e)
    mine = pl.ds(pl.multiple_of(me * tokens, tokens), tokens)

    def columns(place, head):
        return pl.ds(pl.multiple_of((place * heads + head) * HD, HD), HD)

    barrier = pltpu.get_barrier_semaphore()

    def greet(step, carry):
        pl.semaphore_signal(
            barrier, inc=1, device_id={"head": lax.rem(me + step, n)}, device_id_type=MESH
        )
        return carry

    lax.fori_loop(1, n, greet, 0)

    @pl.when(has_next)
    def _():
        pl.semaphore_signal(barrier, inc=1, device_id={"group": group + 1}, device_id_type=MESH)

    @pl.when(group >= 1)
    def _():
        pl.semaphore_signal(barrier, inc=1, device_id={"group": group - 1}, device_id_type=MESH)

    beside = jnp.minimum(group, 1) + jnp.minimum(groups - 1 - group, 1)
    pl.semaphore_wait(barrier, n - 1 + beside)

    def partner(shift):
        if n & (n - 1):
            return lax.rem(me + shift, n)
        bits = [1 << power for power in range(n.bit_length() - 1)]
        return sum((me // bit + shift // bit) % 2 * bit for bit in bits)

    def scatter(head, pairs, send_sem, recv_sem):
        for source, target in pairs:
            pltpu.make_async_copy(
                source.at[0, :, columns(me, head)], target.at[mine, :], recv_sem
            ).start()

        def body(step, carry):
            odd = step % 2
            shift = odd * ((step + 1) // 2) + (1 - odd) * (half + step // 2)
            place = partner(shift)
            for source, target in pairs:
                pltpu.make_async_remote_copy(
                    src_ref=source.at[0, :, columns(place, head)],
                    dst_ref=target.at[mine, :],
                    send_sem=send_sem,
                    recv_sem=recv_sem,
                    device_id={"head": place},
                    device_id_type=MESH,
                ).start()
            return carry

        lax.fori_loop(0, n - 1, body, 0)

    def send_keys(head):
        scatter(
            head,
            ((k_ref, kvbuf.at[head, 0]), (v_ref, kvbuf.at[head, 1])),
            kv_send.at[head],
            kv_recv.at[head],
        )

    def send_queries(head):
        scatter(head, ((q_ref, qbuf.at[head]),), q_send.at[head], q_recv.at[head])

    def wait_sent(head):
        sent = pl.ds(0, (n - 1) * tokens)
        kv = kvbuf.at[head, :, sent, :]
        pltpu.make_async_copy(kv, kv, kv_send.at[head]).wait()
        q = qbuf.at[head, sent, :]
        pltpu.make_async_copy(q, q, q_send.at[head]).wait()

    def hand_on(head, slot):
        return pltpu.make_async_remote_copy(
            src_ref=kvbuf.at[head] if slot == 0 else slots.at[slot - 1, head],
            dst_ref=slots.at[slot, head],
            send_sem=slot_send.at[slot, head],
            recv_sem=slot_recv.at[slot, head],
            device_id={"group": group + 1},
            device_id_type=MESH,
        )

    def prepare(head):
        head_number = me * heads + head
        first_key = kvbuf[head, 0, 0:16, :].astype(jnp.float32)[0:1, :]
        positions = lax.broadcasted_iota(jnp.int32, (seq, HD), 0)
        for offset in range(WIN):
            source = jnp.maximum(group - offset, 0)
            live = jnp.where(
                group >= offset, count_ref[source] * mask_ref[group, source, head_number], 0
            )
            valid = positions < live
            block = kvbuf.at[head] if offset == 0 else slots.at[offset - 1, head]
            rows = pl.ds(offset * seq, seq)
            kall[rows, :] = jnp.where(
                valid, block[0].astype(jnp.float32), first_key
            ).astype(jnp.bfloat16)
            vall[rows, 0:HD] = jnp.where(valid, block[1].astype(jnp.float32), 0.0).astype(
                jnp.bfloat16
            )
            vall[rows, HD : 2 * HD] = jnp.where(valid, 1.0, 0.0).astype(jnp.bfloat16)

    def attend(head, first, last):
        gates = gate_ref[:, columns(me, head)]
        levels = lax.broadcasted_iota(jnp.int32, gates.shape, 0)
        gate = jnp.sum(
            jnp.where(levels == level_ref[group], gates, 0.0), axis=0, keepdims=True
        )

        def body(step, carry):
            index = lax.rem(step + me // per + n_tiles // 2, n_tiles)
            start = pl.multiple_of(index * tile, tile)
            rows = qbuf[head, pl.ds(start, tile), :]
            tops, sums = [], []
            for offset in range(WIN):
                keys = pl.ds(offset * seq, seq)
                scores = lax.dot_general(
                    rows, kall[keys, :], (((1,), (1,)), ((), ())),
                    preferred_element_type=jnp.float32,
                )
                top = jnp.max(scores, axis=1, keepdims=True)
                weights = jnp.exp2((scores - top) * scale).astype(jnp.bfloat16)
                tops.append(top)
                sums.append(jnp.dot(weights, vall[keys, :], preferred_element_type=jnp.float32))
            joint = functools.reduce(jnp.maximum, tops)
            summed = sum(
                jnp.exp2((top - joint) * scale) * part for top, part in zip(tops, sums)
            )
            gated = summed[:, 0:HD] / summed[:, HD : 2 * HD] * gate
            obuf[head, pl.ds(start, tile), :] = gated.astype(jnp.bfloat16)
            for piece in range(per):
                place = index * per + piece
                piece_rows = pl.ds(pl.multiple_of(place * tokens, tokens), tokens)
                finished = obuf.at[head, piece_rows, :]
                landing = out_ref.at[0, :, columns(me, head)]

                @pl.when(place == me)
                def _():
                    pltpu.make_async_copy(finished, landing, out_recv).start()

                @pl.when(place != me)
                def _():
                    pltpu.make_async_remote_copy(
                        src_ref=finished,
                        dst_ref=landing,
                        send_sem=out_send,
                        recv_sem=out_recv,
                        device_id={"head": place},
                        device_id_type=MESH,
                    ).start()

            return carry

        lax.fori_loop(first, last, body, 0)

    send_keys(0)
    for head in range(heads):
        if head + 1 < heads:
            send_keys(head + 1)
        send_queries(head)
    for stage in range(heads + 1):
        head = stage - 1
        if stage < heads:
            pltpu.make_async_copy(kvbuf.at[stage], kvbuf.at[stage], kv_recv.at[stage]).wait()

            @pl.when(has_next)
            def _():
                hand_on(stage, 0).start()

        if stage >= 1:
            pltpu.make_async_copy(qbuf.at[head], qbuf.at[head], q_recv.at[head]).wait()

            @pl.when(group >= 2)
            def _():
                hand_on(head, 1).wait_recv()

            prepare(head)
            attend(head, 0, n_tiles // 2)

        if stage < heads:

            @pl.when(group >= 1)
            def _():
                hand_on(stage, 0).wait_recv()

                @pl.when(has_next)
                def _():
                    hand_on(stage, 1).start()

        if stage >= 1:
            attend(head, n_tiles // 2, n_tiles)

    for head in range(heads):
        wait_sent(head)

        @pl.when(has_next)
        def _():
            hand_on(head, 0).wait_send()

            @pl.when(group >= 1)
            def _():
                hand_on(head, 1).wait_send()

    sent = obuf.at[:, pl.ds(0, (n - 1) * tokens), :]
    pltpu.make_async_copy(sent, sent, out_send).wait()
    pltpu.make_async_copy(out_ref, out_ref, out_recv).wait()


def solution(mesh):
    n = mesh.shape["head"]
    groups = mesh.shape["group"]

    def shards(queries, keys, values, group_mask, noise_level, token_count, level_gate):
        _, tokens, features = queries.shape
        heads = features // HD // n
        seq = tokens * n
        tile = max(tokens, 256 if seq <= 1024 else 128)
        any_space = pl.BlockSpec(memory_space=pl.ANY)
        smem = pl.BlockSpec(memory_space=pltpu.SMEM)
        dma = pltpu.SemaphoreType.DMA
        scores = heads * seq * seq * WIN
        return pl.pallas_call(
            functools.partial(kernel, n, groups, tile),
            out_shape=jax.ShapeDtypeStruct(queries.shape, jnp.bfloat16),
            in_specs=[any_space] * 3 + [smem] * 3 + [pl.BlockSpec(memory_space=pltpu.VMEM)],
            out_specs=any_space,
            scratch_shapes=[
                pltpu.VMEM((heads, seq, HD), jnp.bfloat16),
                pltpu.VMEM((heads, 2, seq, HD), jnp.bfloat16),
                pltpu.VMEM((WIN - 1, heads, 2, seq, HD), jnp.bfloat16),
                pltpu.VMEM((WIN * seq, HD), jnp.bfloat16),
                pltpu.VMEM((WIN * seq, 2 * HD), jnp.bfloat16),
                pltpu.VMEM((heads, seq, HD), jnp.bfloat16),
                dma((heads,)),
                dma((heads,)),
                dma((heads,)),
                dma((heads,)),
                dma((WIN - 1, heads)),
                dma((WIN - 1, heads)),
                dma,
                dma,
            ],
            compiler_params=pltpu.CompilerParams(
                collective_id=0, has_side_effects=True, vmem_limit_bytes=56 * 1024 * 1024
            ),
            cost_estimate=pl.CostEstimate(
                flops=scores * HD * 4, bytes_accessed=queries.size * 8, transcendentals=scores
            ),
        )(queries, keys, values, group_mask, noise_level, token_count, level_gate)

    return jax.shard_map(
        shards,
        mesh=mesh,
        in_specs=(P("group", "head", None),) * 3 + (P(),) * 4,
        out_specs=P("group", "head", None),
        check_vma=False,
    )
```

```python
import functools
import math

import jax
import jax.numpy as jnp
from jax import lax
from jax.experimental import pallas as pl
from jax.experimental.pallas import tpu as pltpu
from jax.sharding import PartitionSpec as P

HD = 128
WIN = 3
MESH = pl.DeviceIdType.MESH


def kernel(
    n, groups, tile,
    q_ref, k_ref, v_ref, mask_ref, level_ref, count_ref, gate_ref, out_ref,
    qbuf, kvbuf, slots, kall, vall, obuf,
    kv_send, kv_recv, q_send, q_recv, slot_send, slot_recv, out_send, out_recv,
):
    group = lax.axis_index("group")
    me = lax.axis_index("head")
    heads, seq, _ = qbuf.shape
    tokens = seq // n
    half = n // 2
    has_next = group < groups - 1
    per = tile // tokens
    n_tiles = seq // tile
    scale = HD ** -0.5 * math.log2(math.e)
    mine = pl.ds(pl.multiple_of(me * tokens, tokens), tokens)

    def columns(place, head):
        return pl.ds(pl.multiple_of((place * heads + head) * HD, HD), HD)

    barrier = pltpu.get_barrier_semaphore()

    def greet(step, carry):
        pl.semaphore_signal(
            barrier, inc=1, device_id={"head": lax.rem(me + step, n)}, device_id_type=MESH
        )
        return carry

    lax.fori_loop(1, n, greet, 0)

    @pl.when(has_next)
    def _():
        pl.semaphore_signal(barrier, inc=1, device_id={"group": group + 1}, device_id_type=MESH)

    @pl.when(group >= 1)
    def _():
        pl.semaphore_signal(barrier, inc=1, device_id={"group": group - 1}, device_id_type=MESH)

    beside = jnp.minimum(group, 1) + jnp.minimum(groups - 1 - group, 1)
    pl.semaphore_wait(barrier, n - 1 + beside)

    def partner(shift):
        if n & (n - 1):
            return lax.rem(me + shift, n)
        bits = [1 << power for power in range(n.bit_length() - 1)]
        return sum((me // bit + shift // bit) % 2 * bit for bit in bits)

    def scatter(head, pairs, send_sem, recv_sem):
        for source, target in pairs:
            pltpu.make_async_copy(
                source.at[0, :, columns(me, head)], target.at[mine, :], recv_sem
            ).start()

        def body(step, carry):
            odd = step % 2
            shift = odd * ((step + 1) // 2) + (1 - odd) * (half + step // 2)
            place = partner(shift)
            for source, target in pairs:
                pltpu.make_async_remote_copy(
                    src_ref=source.at[0, :, columns(place, head)],
                    dst_ref=target.at[mine, :],
                    send_sem=send_sem,
                    recv_sem=recv_sem,
                    device_id={"head": place},
                    device_id_type=MESH,
                ).start()
            return carry

        lax.fori_loop(0, n - 1, body, 0)

    def send_keys(head):
        scatter(
            head,
            ((k_ref, kvbuf.at[head, 0]), (v_ref, kvbuf.at[head, 1])),
            kv_send.at[head],
            kv_recv.at[head],
        )

    def send_queries(head):
        scatter(head, ((q_ref, qbuf.at[head]),), q_send.at[head], q_recv.at[head])

    def wait_sent(head):
        sent = pl.ds(0, (n - 1) * tokens)
        kv = kvbuf.at[head, :, sent, :]
        pltpu.make_async_copy(kv, kv, kv_send.at[head]).wait()
        q = qbuf.at[head, sent, :]
        pltpu.make_async_copy(q, q, q_send.at[head]).wait()

    def hand_on(head, slot):
        return pltpu.make_async_remote_copy(
            src_ref=kvbuf.at[head] if slot == 0 else slots.at[slot - 1, head],
            dst_ref=slots.at[slot, head],
            send_sem=slot_send.at[slot, head],
            recv_sem=slot_recv.at[slot, head],
            device_id={"group": group + 1},
            device_id_type=MESH,
        )

    def prepare(head):
        head_number = me * heads + head
        first_key = kvbuf[head, 0, 0:16, :].astype(jnp.float32)[0:1, :]
        positions = lax.broadcasted_iota(jnp.int32, (seq, HD), 0)
        for offset in range(WIN):
            source = jnp.maximum(group - offset, 0)
            live = jnp.where(
                group >= offset, count_ref[source] * mask_ref[group, source, head_number], 0
            )
            valid = positions < live
            block = kvbuf.at[head] if offset == 0 else slots.at[offset - 1, head]
            rows = pl.ds(offset * seq, seq)
            kall[rows, :] = jnp.where(
                valid, block[0].astype(jnp.float32), first_key
            ).astype(jnp.bfloat16)
            vall[rows, 0:HD] = jnp.where(valid, block[1].astype(jnp.float32), 0.0).astype(
                jnp.bfloat16
            )
            vall[rows, HD : 2 * HD] = jnp.where(valid, 1.0, 0.0).astype(jnp.bfloat16)

    def attend(head, first, last):
        if head + 2 < heads:
            attend_blocks(head, first, last, WIN)
            return
        reach = jnp.minimum(group, WIN - 1)
        for blocks in range(1, WIN + 1):

            @pl.when(reach == blocks - 1)
            def _():
                attend_blocks(head, first, last, blocks)

    def attend_blocks(head, first, last, blocks):
        gates = gate_ref[:, columns(me, head)]
        levels = lax.broadcasted_iota(jnp.int32, gates.shape, 0)
        gate = jnp.sum(
            jnp.where(levels == level_ref[group], gates, 0.0), axis=0, keepdims=True
        )

        def body(step, carry):
            index = lax.rem(step + me // per + n_tiles // 2, n_tiles)
            start = pl.multiple_of(index * tile, tile)
            rows = qbuf[head, pl.ds(start, tile), :]
            tops, sums = [], []
            for offset in range(blocks):
                keys = pl.ds(offset * seq, seq)
                scores = lax.dot_general(
                    rows, kall[keys, :], (((1,), (1,)), ((), ())),
                    preferred_element_type=jnp.float32,
                )
                top = jnp.max(scores, axis=1, keepdims=True)
                weights = jnp.exp2((scores - top) * scale).astype(jnp.bfloat16)
                tops.append(top)
                sums.append(jnp.dot(weights, vall[keys, :], preferred_element_type=jnp.float32))
            joint = functools.reduce(jnp.maximum, tops)
            summed = sum(
                jnp.exp2((top - joint) * scale) * part for top, part in zip(tops, sums)
            )
            gated = summed[:, 0:HD] / summed[:, HD : 2 * HD] * gate
            obuf[head, pl.ds(start, tile), :] = gated.astype(jnp.bfloat16)
            for piece in range(per):
                place = index * per + piece
                piece_rows = pl.ds(pl.multiple_of(place * tokens, tokens), tokens)
                finished = obuf.at[head, piece_rows, :]
                landing = out_ref.at[0, :, columns(me, head)]

                @pl.when(place == me)
                def _():
                    pltpu.make_async_copy(finished, landing, out_recv).start()

                @pl.when(place != me)
                def _():
                    pltpu.make_async_remote_copy(
                        src_ref=finished,
                        dst_ref=landing,
                        send_sem=out_send,
                        recv_sem=out_recv,
                        device_id={"head": place},
                        device_id_type=MESH,
                    ).start()

            return carry

        lax.fori_loop(first, last, body, 0)

    send_keys(0)
    for head in range(heads):
        if head + 1 < heads:
            send_keys(head + 1)
        send_queries(head)
    for stage in range(heads + 1):
        head = stage - 1
        if stage < heads:
            pltpu.make_async_copy(kvbuf.at[stage], kvbuf.at[stage], kv_recv.at[stage]).wait()

            @pl.when(has_next)
            def _():
                hand_on(stage, 0).start()

        if stage >= 1:
            pltpu.make_async_copy(qbuf.at[head], qbuf.at[head], q_recv.at[head]).wait()

            @pl.when(group >= 2)
            def _():
                hand_on(head, 1).wait_recv()

            prepare(head)
            attend(head, 0, n_tiles // 2 if stage < heads else n_tiles)

        if stage < heads:

            @pl.when(group >= 1)
            def _():
                hand_on(stage, 0).wait_recv()

                @pl.when(has_next)
                def _():
                    hand_on(stage, 1).start()

            if stage >= 1:
                attend(head, n_tiles // 2, n_tiles)

    for head in range(heads):
        wait_sent(head)

        @pl.when(has_next)
        def _():
            hand_on(head, 0).wait_send()

            @pl.when(group >= 1)
            def _():
                hand_on(head, 1).wait_send()

    sent = obuf.at[:, pl.ds(0, (n - 1) * tokens), :]
    pltpu.make_async_copy(sent, sent, out_send).wait()
    pltpu.make_async_copy(out_ref, out_ref, out_recv).wait()


def solution(mesh):
    n = mesh.shape["head"]
    groups = mesh.shape["group"]

    def shards(queries, keys, values, group_mask, noise_level, token_count, level_gate):
        _, tokens, features = queries.shape
        heads = features // HD // n
        seq = tokens * n
        tile = max(tokens, 256 if seq <= 1024 else 128)
        any_space = pl.BlockSpec(memory_space=pl.ANY)
        smem = pl.BlockSpec(memory_space=pltpu.SMEM)
        dma = pltpu.SemaphoreType.DMA
        scores = heads * seq * seq * WIN
        return pl.pallas_call(
            functools.partial(kernel, n, groups, tile),
            out_shape=jax.ShapeDtypeStruct(queries.shape, jnp.bfloat16),
            in_specs=[any_space] * 3 + [smem] * 3 + [pl.BlockSpec(memory_space=pltpu.VMEM)],
            out_specs=any_space,
            scratch_shapes=[
                pltpu.VMEM((heads, seq, HD), jnp.bfloat16),
                pltpu.VMEM((heads, 2, seq, HD), jnp.bfloat16),
                pltpu.VMEM((WIN - 1, heads, 2, seq, HD), jnp.bfloat16),
                pltpu.VMEM((WIN * seq, HD), jnp.bfloat16),
                pltpu.VMEM((WIN * seq, 2 * HD), jnp.bfloat16),
                pltpu.VMEM((heads, seq, HD), jnp.bfloat16),
                dma((heads,)),
                dma((heads,)),
                dma((heads,)),
                dma((heads,)),
                dma((WIN - 1, heads)),
                dma((WIN - 1, heads)),
                dma,
                dma,
            ],
            compiler_params=pltpu.CompilerParams(
                collective_id=0, has_side_effects=True, vmem_limit_bytes=56 * 1024 * 1024
            ),
            cost_estimate=pl.CostEstimate(
                flops=scores * HD * 4, bytes_accessed=queries.size * 8, transcendentals=scores
            ),
        )(queries, keys, values, group_mask, noise_level, token_count, level_gate)

    return jax.shard_map(
        shards,
        mesh=mesh,
        in_specs=(P("group", "head", None),) * 3 + (P(),) * 4,
        out_specs=P("group", "head", None),
        check_vma=False,
    )
```
